32 devices in a mesh: tm: 8 (over y, x, core), pen: 4 (over z).
Axes of the slice: x: 2, y: 2, z: 4, core: 2. Of those that a mesh axis runs over, the one named last changes fastest.
Arguments:
- clips: bfloat16 [4, 16384, 256], P('pen', 'tm'), may hold values from -6 to 6
- targets: bfloat16 [4, 16384, 1024], P('pen', 'tm'), may hold values from -6 to 6
- conv_weight: bfloat16 [3, 3, 256, 256], replicated, may hold values from -0.21875 to 0.21875
- head_weight: bfloat16 [256, 1024], replicated, may hold values from -0.375 to 0.375
Outputs:
- conv_grad: float32 [3, 3, 256, 256], P(None, None, 'pen')
- head_grad: float32 [256, 1024], P('pen')
The draws below stay inside these ranges and needn't reach their ends.
All inputs are finite; a program needn't handle non-finite values.
Results may differ from the reference program's by a relative error of at most 0.00031.
Values may be sent and summed in bfloat16 or wider, within the bound.
No kernel may reach another device: no remote copies, remote signals or barrier semaphores. Data moves between devices by JAX's collectives and lax.ppermute only.
A program may use at most 128 MiB of HBM per device.

```python
import jax
import jax.numpy as jnp
from jax import lax

W = 256
FEAT = 1024
D1 = 16
D2 = 64
D3 = 256
FRAMES = 16384
PENS = 4


def level_of(rng, extent, split, least, largest):
    loudness, own = 1.0, jax.random.fold_in(rng, 6)
    for axis_at, blocks in split:
        draws = jnp.exp(jax.random.uniform(jax.random.fold_in(own, axis_at), (blocks,), jnp.float32, least / len(split), largest / len(split)))
        loudness = loudness * jnp.repeat(draws, extent[axis_at] // blocks).reshape([-1 if axis == axis_at else 1 for axis in range(len(extent))])
    return loudness


def centred(own_key, dims, scale, reach, shards=(), dtype=jnp.bfloat16):
    values = jax.random.normal(own_key, dims, jnp.float32) * scale
    if len(shards) > 0:
        values = level_of(own_key, dims, shards, -0.22, 0.18) * values
    return jnp.clip(values, min=-reach, max=reach).astype(dtype)


def setup_inputs(seed: int = 0) -> dict:
    key_list = jax.random.split(jax.random.key(seed), 5)
    clips = centred(key_list[0], (PENS, FRAMES, W), 1.0, 6.0, ((0, 4), (1, 8)))
    targets = centred(key_list[1], (PENS, FRAMES, FEAT), 1.0, 6.0, ((0, 4), (1, 8)))
    conv_weight = centred(key_list[2], (3, 3, W, W), (3 * W) ** -0.5, 0.21875)
    head_weight = centred(key_list[3], (W, FEAT), W ** -0.5, 0.375)
    return {"clips": clips, "targets": targets, "conv_weight": conv_weight, "head_weight": head_weight}


def trans_dot(left, right):
    return lax.dot_general(left.astype(jnp.float32), right.astype(jnp.float32), (((0,), (0,)), ((), ())), precision=lax.Precision.HIGHEST, preferred_element_type=jnp.float32)


def full_dot(left, right):
    return jnp.dot(left.astype(jnp.float32), right.astype(jnp.float32), precision=lax.Precision.HIGHEST, preferred_element_type=jnp.float32)


def stream_grads(pair, conv_weight, head_weight):
    clip, target = pair
    count = clip.shape[0]
    dilations = (D1, D2, D3)
    hidden = clip
    saved = []
    for layer in range(3):
        width = dilations[layer]
        padded = jnp.pad(hidden, ((width, width), (0, 0)))
        pre = jnp.dot(padded[0:count], conv_weight[layer, 0], preferred_element_type=jnp.float32)
        pre = pre + jnp.dot(padded[width:width + count], conv_weight[layer, 1], preferred_element_type=jnp.float32)
        pre = pre + jnp.dot(padded[2 * width:2 * width + count], conv_weight[layer, 2], preferred_element_type=jnp.float32)
        saved.append((padded, pre))
        hidden = (hidden.astype(jnp.float32) + jax.nn.silu(pre)).astype(jnp.bfloat16)
    pred = jnp.dot(hidden, head_weight, preferred_element_type=jnp.float32)
    grad_pred = (pred - target.astype(jnp.float32)) * (2.0 / FEAT)
    head_grad = trans_dot(hidden, grad_pred)
    error = full_dot(grad_pred, head_weight.T)
    layer_grads = [None, None, None]
    for layer in (2, 1, 0):
        width = dilations[layer]
        padded, pre = saved[layer]
        sig = jax.nn.sigmoid(pre)
        back = error * sig * (1.0 + pre * (1.0 - sig))
        taps = [trans_dot(padded[k * width:k * width + count], back) for k in range(3)]
        layer_grads[layer] = jnp.stack(taps)
        if layer > 0:
            back_pad = jnp.pad(back, ((width, width), (0, 0)))
            for k in range(3):
                start = (2 - k) * width
                error = error + full_dot(back_pad[start:start + count], conv_weight[layer, k].T)
    return jnp.stack(layer_grads), head_grad


def reference(clips, targets, conv_weight, head_weight):
    conv_all, head_all = lax.map(lambda pair: stream_grads(pair, conv_weight, head_weight), (clips, targets))
    return jnp.sum(conv_all, axis=0), jnp.sum(head_all, axis=0)
```

```python
import functools

import jax
import jax.numpy as jnp
from jax import lax
from jax.experimental import pallas as pl
from jax.experimental.pallas import tpu as pltpu
from jax.sharding import PartitionSpec as P

W = 256
FEAT = 1024
DILATIONS = (16, 64, 256)
BACK = DILATIONS[1] + DILATIONS[2]
HALO = BACK + sum(DILATIONS)
SCALE = 2.0 / FEAT
SUM_LANES = 9 * W + FEAT


def dot(left, right):
    return lax.dot_general(
        left, right, (((1,), (0,)), ((), ())), preferred_element_type=jnp.float32
    )


def dot_nt(left, right):
    return lax.dot_general(
        left, right, (((1,), (1,)), ((), ())), preferred_element_type=jnp.float32
    )


def dot_tn(left, right):
    return lax.dot_general(
        left, right, (((0,), (0,)), ((), ())), preferred_element_type=jnp.float32
    )


def split(value):
    high = value.astype(jnp.bfloat16)
    return high, (value - high.astype(jnp.float32)).astype(jnp.bfloat16)


def tile_of(rows, most):
    best = 16
    for size in range(16, most + 1, 16):
        if rows % size == 0:
            best = size
    return best


def project_kernel(target_ref, head_ref, out_ref):
    out_ref[...] = dot_nt(target_ref[...], head_ref[...])


def project(target, head_weight):
    count = target.shape[0]
    tile = tile_of(count, 512)
    return pl.pallas_call(
        project_kernel,
        grid=(count // tile,),
        in_specs=[
            pl.BlockSpec((tile, FEAT), lambda i: (i, 0)),
            pl.BlockSpec((W, FEAT), lambda i: (0, 0)),
        ],
        out_specs=pl.BlockSpec((tile, W), lambda i: (i, 0)),
        out_shape=jax.ShapeDtypeStruct((count, W), jnp.float32),
        cost_estimate=pl.CostEstimate(
            flops=2 * count * W * FEAT, bytes_accessed=count * (2 * FEAT + 4 * W), transcendentals=0
        ),
        name="project_targets",
    )(target, head_weight)


def loop_rows(start, stop, most, body):
    tile = tile_of(stop - start, most)

    def step(index, carry):
        body(index * tile + start, tile)
        return carry

    lax.fori_loop(0, (stop - start) // tile, step, 0)


def main_kernel(
    count,
    place_ref,
    clip_ref,
    clip_a_ref,
    clip_b_ref,
    target_ref,
    proj_ref,
    proj_a_ref,
    proj_b_ref,
    conv_ref,
    head_ref,
    out_ref,
    h0,
    h1,
    h2,
    h3,
    s1,
    s2,
    s3,
    err,
    back,
    conv_t,
    gram,
    head_acc,
):
    first = place_ref[0] == 0
    last = place_ref[0] == place_ref[1] - 1
    even = place_ref[0] % 2 == 0
    hidden = (h0, h1, h2, h3)
    slopes = (None, s1, s2, s3)

    def at(frame, size):
        return pl.ds(pl.multiple_of(frame + HALO, 16), size)

    def inside(frame, size):
        rows = lax.broadcasted_iota(jnp.int32, (size, 1), 0) + frame
        return ((rows >= 0) | jnp.logical_not(first)) & ((rows < count) | jnp.logical_not(last))

    h0[HALO : HALO + count, :] = clip_ref[...]
    err[HALO : HALO + count, :] = proj_ref[...]

    @pl.when(even)
    def _():
        h0[0:HALO, :] = clip_b_ref[...]
        h0[HALO + count :, :] = clip_a_ref[...]
        err[HALO - BACK : HALO, :] = proj_b_ref[...]
        err[HALO + count : HALO + count + BACK, :] = proj_a_ref[...]

    @pl.when(jnp.logical_not(even))
    def _():
        h0[0:HALO, :] = clip_a_ref[...]
        h0[HALO + count :, :] = clip_b_ref[...]
        err[HALO - BACK : HALO, :] = proj_a_ref[...]
        err[HALO + count : HALO + count + BACK, :] = proj_b_ref[...]

    for layer in (1, 2):
        for k in range(3):
            turned = jnp.transpose(conv_ref[layer, k])
            conv_t[layer - 1, 2 * k * W : (2 * k + 1) * W, :] = turned
            conv_t[layer - 1, (2 * k + 1) * W : (2 * k + 2) * W, :] = turned
    high, low = split(dot_nt(head_ref[...], head_ref[...]))
    gram[0:W, :] = high
    gram[W : 2 * W, :] = low

    reach = HALO
    for layer in range(3):
        width = DILATIONS[layer]
        reach -= width
        source, result, slope = hidden[layer], hidden[layer + 1], slopes[layer + 1]
        weights = conv_ref[layer].reshape(3 * W, W)

        def forward(frame, size):
            taps = [source[at(frame + (k - 1) * width, size), :] for k in range(3)]
            pre = dot(jnp.concatenate(taps, axis=1), weights)
            sig = 0.5 * jnp.tanh(0.5 * pre) + 0.5
            new = taps[1].astype(jnp.float32) + pre * sig
            result[at(frame, size), :] = jnp.where(inside(frame, size), new, 0.0).astype(jnp.bfloat16)
            slope[at(frame, size), :] = sig * (1.0 + pre * (1.0 - sig))

        loop_rows(-reach, count + reach, 416, forward)

    def store_back(frame, size, error, slope):
        high, low = split(error * slope[at(frame, size), :])
        back[at(frame, size), 0:W] = high
        back[at(frame, size), W : 2 * W] = low

    def head_error(frame, size):
        top = h3[at(frame, size), :]
        error = SCALE * (dot(jnp.concatenate([top, top], axis=1), gram[...]) - err[at(frame, size), :])
        err[at(frame, size), :] = error
        store_back(frame, size, error, s3)

    loop_rows(-BACK, count + BACK, 416, head_error)

    head_acc[...] = jnp.zeros_like(head_acc)

    def head_sum(frame, size):
        top = h3[at(frame, size), :]
        goal = target_ref[pl.ds(pl.multiple_of(frame, 16), size), :]
        head_acc[...] += dot_tn(top, jnp.concatenate([goal, top], axis=1))

    loop_rows(0, count, 512, head_sum)
    square = head_acc[:, FEAT:]
    high = square.astype(jnp.bfloat16)
    middle, low = split(square - high.astype(jnp.float32))
    weight = head_ref[...]
    product = dot(high, weight) + (dot(middle, weight) + dot(low, weight))
    out_ref[:, 9 * W :] = SCALE * (product - head_acc[:, 0:FEAT])

    reach = BACK
    for layer in (2, 1, 0):
        width = DILATIONS[layer]
        source = hidden[layer]
        first_lane = 3 * layer * W
        out_ref[:, first_lane : first_lane + 3 * W] = jnp.zeros((W, 3 * W), jnp.float32)

        def weight_sum(frame, size):
            right = back[at(frame, size), :]
            for k in range(3):
                both = dot_tn(source[at(frame + (k - 1) * width, size), :], right)
                lanes = pl.ds(first_lane + k * W, W)
                out_ref[:, lanes] += both[:, 0:W] + both[:, W:]

        loop_rows(0, count, 512, weight_sum)
        if layer > 0:
            reach -= width

            def pull_back(frame, size):
                taps = [back[at(frame - (k - 1) * width, size), :] for k in range(3)]
                err[at(frame, size), :] += dot(jnp.concatenate(taps, axis=1), conv_t[layer - 1])

            loop_rows(-reach, count + reach, 416, pull_back)

            def slope_back(frame, size):
                error = jnp.where(inside(frame, size), err[at(frame, size), :], 0.0)
                store_back(frame, size, error, slopes[layer])

            loop_rows(-reach, count + reach, 416, slope_back)


def main(place, clip, clip_a, clip_b, target, proj, proj_a, proj_b, conv_weight, head_weight):
    count = clip.shape[0]
    rows = count + 2 * HALO
    vmem = pl.BlockSpec(memory_space=pltpu.VMEM)
    flops = 2 * W * W * (9 * rows + 14 * rows + 18 * count + 6 * count)
    return pl.pallas_call(
        functools.partial(main_kernel, count),
        in_specs=[pl.BlockSpec(memory_space=pltpu.SMEM)] + [vmem] * 9,
        out_specs=vmem,
        out_shape=jax.ShapeDtypeStruct((W, SUM_LANES), jnp.float32),
        scratch_shapes=[pltpu.VMEM((rows, W), jnp.bfloat16)] * 4
        + [pltpu.VMEM((rows, W), jnp.float32)] * 4
        + [
            pltpu.VMEM((rows, 2 * W), jnp.bfloat16),
            pltpu.VMEM((2, 6 * W, W), jnp.bfloat16),
            pltpu.VMEM((2 * W, W), jnp.bfloat16),
            pltpu.VMEM((W, FEAT + W), jnp.float32),
        ],
        compiler_params=pltpu.CompilerParams(vmem_limit_bytes=56 * 2**20),
        cost_estimate=pl.CostEstimate(flops=flops, bytes_accessed=16 * 2**20, transcendentals=3 * rows * W),
        name="forward_backward",
    )(place, clip, clip_a, clip_b, target, proj, proj_a, proj_b, conv_weight, head_weight)


def edges(block, width):
    count = lax.axis_size("tm")
    even = lax.axis_index("tm") % 2 == 0
    low, high = block[:width], block[block.shape[0] - width :]
    near = [(i, i ^ 1) for i in range(count)]
    far = [(i, i + 1) for i in range(1, count - 1, 2)]
    far = far + [(j, i) for i, j in far]
    from_far = lax.ppermute(jnp.where(even, low, high), "tm", far)
    from_near = lax.ppermute(jnp.where(even, high, low), "tm", near)
    return from_near, from_far


def pick(array, index, axis):
    return lax.dynamic_index_in_dim(array, index, axis, keepdims=False)


def reduce_rows(total):
    n, pens = lax.axis_size("tm"), lax.axis_size("pen")
    place, pen = lax.axis_index("tm"), lax.axis_index("pen")
    core, group, groups = place % 2, place // 2, n // 2
    part = total.reshape(pens, 2, groups, total.shape[0] // (pens * n), total.shape[1])
    other = lax.ppermute(pick(part, 1 - core, 1), "tm", [(i, i ^ 1) for i in range(n)])
    part = pick(part, core, 1) + other
    arrived = [
        lax.ppermute(pick(part, group ^ j, 1), "tm", [(i, i ^ (2 * j)) for i in range(n)])
        for j in range(1, groups)
    ]
    part = pick(part, group, 1)
    for other in arrived:
        part = part + other
    arrived = [
        lax.ppermute(pick(part, pen ^ j, 0), "pen", [(i, i ^ j) for i in range(pens)])
        for j in range(1, pens)
    ]
    part = pick(part, pen, 0)
    for other in arrived:
        part = part + other
    return part


def gather_rows(part):
    n = lax.axis_size("tm")
    place = lax.axis_index("tm")
    core, group, groups = place % 2, place // 2, n // 2
    half = jnp.zeros((groups,) + part.shape, part.dtype)
    half = lax.dynamic_update_index_in_dim(half, part, group, 0)
    for j in range(1, groups):
        other = lax.ppermute(part, "tm", [(i, i ^ (2 * j)) for i in range(n)])
        half = lax.dynamic_update_index_in_dim(half, other, group ^ j, 0)
    half = half.reshape((-1,) + part.shape[1:])
    other = lax.ppermute(half, "tm", [(i, i ^ 1) for i in range(n)])
    return jnp.concatenate([jnp.where(core == 0, half, other), jnp.where(core == 0, other, half)], axis=0)


def on_device(clips, targets, conv_weight, head_weight):
    clip, target = clips[0], targets[0]
    place = jnp.stack([lax.axis_index("tm"), lax.axis_size("tm")]).astype(jnp.int32)
    clip_a, clip_b = edges(clip, HALO)
    proj = project(target, head_weight)
    proj_a, proj_b = edges(proj, BACK)
    total = main(place, clip, clip_a, clip_b, target, proj, proj_a, proj_b, conv_weight, head_weight)
    mine = gather_rows(reduce_rows(total))
    conv = mine[:, : 9 * W].reshape(-1, 3, 3, W).transpose(1, 2, 0, 3)
    return conv, mine[:, 9 * W :]


def solution(mesh):
    in_specs = (P("pen", "tm", None), P("pen", "tm", None), P(), P())
    out_specs = (P(None, None, "pen", None), P("pen", None))
    return jax.shard_map(
        on_device, mesh=mesh, in_specs=in_specs, out_specs=out_specs, check_vma=False
    )
```

```python
import functools
import math

import jax
import jax.numpy as jnp
from jax import lax
from jax.experimental import pallas as pl
from jax.experimental.pallas import tpu as pltpu
from jax.sharding import PartitionSpec as P

W = 256
FEAT = 1024
DILATIONS = (16, 64, 256)
BACK = DILATIONS[1] + DILATIONS[2]
HALO = BACK + sum(DILATIONS)
SCALE = 2.0 / FEAT
SUM_LANES = 9 * W + FEAT
GROUPS = ((0, 3 * W), (3 * W, 6 * W), (6 * W, 9 * W), (9 * W, SUM_LANES))
CODE_LANES = SUM_LANES + 128
BASE = 125.0 * math.log(2.0)
SPAN = 250.0 * math.log(2.0)


def dot(left, right):
    return lax.dot_general(
        left, right, (((1,), (0,)), ((), ())), preferred_element_type=jnp.float32
    )


def dot_nt(left, right):
    return lax.dot_general(
        left, right, (((1,), (1,)), ((), ())), preferred_element_type=jnp.float32
    )


def dot_tn(left, right):
    return lax.dot_general(
        left, right, (((0,), (0,)), ((), ())), preferred_element_type=jnp.float32
    )


def split(value):
    high = value.astype(jnp.bfloat16)
    return high, (value - high.astype(jnp.float32)).astype(jnp.bfloat16)


def tile_of(rows, most):
    best = 16
    for size in range(16, most + 1, 16):
        if rows % size == 0:
            best = size
    return best


def loop_rows(start, stop, most, body):
    tile = tile_of(stop - start, most)
    for frame in range(start, stop, tile):
        body(frame, tile)


def project_kernel(place_ref, target_ref, head_ref, out_ref, near_ref, far_ref):
    count = target_ref.shape[0]
    low, high = slice(0, BACK), slice(count - BACK, count)
    even = place_ref[0] % 2 == 0
    loop_rows(0, count, 512, functools.partial(project_rows, target_ref, head_ref, out_ref))

    @pl.when(even)
    def _():
        near_ref[...] = out_ref[high, :]
        far_ref[...] = out_ref[low, :]

    @pl.when(jnp.logical_not(even))
    def _():
        near_ref[...] = out_ref[low, :]
        far_ref[...] = out_ref[high, :]


def project_rows(target_ref, head_ref, out_ref, frame, size):
    out_ref[frame : frame + size, :] = dot_nt(target_ref[frame : frame + size, :], head_ref[...])


def project(place, target, head_weight):
    count = target.shape[0]
    return pl.pallas_call(
        project_kernel,
        in_specs=[smem(), whole(), whole()],
        out_specs=[whole()] * 3,
        out_shape=[jax.ShapeDtypeStruct((rows, W), jnp.float32) for rows in (count, BACK, BACK)],
        compiler_params=pltpu.CompilerParams(vmem_limit_bytes=24 * 2**20),
        cost_estimate=pl.CostEstimate(
            flops=2 * count * W * FEAT, bytes_accessed=count * (2 * FEAT + 4 * W), transcendentals=0
        ),
        name="project_targets",
    )(place, target, head_weight)


def main_kernel(
    count,
    place_ref,
    clip_ref,
    clip_a_ref,
    clip_b_ref,
    target_hbm,
    proj_ref,
    proj_a_ref,
    proj_b_ref,
    conv_hbm,
    head_hbm,
    keep_ref,
    send_ref,
    h0,
    h1,
    h2,
    h3,
    s1,
    s2,
    s3,
    err,
    back,
    conv_t,
    gram,
    head_acc,
    sums,
    conv_ref,
    head_ref,
    target_ref,
    in_sem,
    out_sem,
):
    first = place_ref[0] == 0
    last = place_ref[0] == place_ref[1] - 1
    even = place_ref[0] % 2 == 0
    hidden = (h0, h1, h2, h3)
    slopes = (None, s1, s2, s3)

    def at(frame, size):
        return slice(frame + HALO, frame + HALO + size)

    def inside(frame, size):
        rows = lax.broadcasted_iota(jnp.int32, (size, 1), 0) + frame
        return ((rows >= 0) | jnp.logical_not(first)) & ((rows < count) | jnp.logical_not(last))

    def masked(frame, size, value):
        if frame >= 0 and frame + size <= count:
            return value
        return jnp.where(inside(frame, size), value, 0.0)

    above = pl.multiple_of(jnp.where(even, HALO + count, 0), 16)
    below = pl.multiple_of(jnp.where(even, 0, HALO + count), 16)
    err_above = pl.multiple_of(jnp.where(even, HALO + count, HALO - BACK), 16)
    err_below = pl.multiple_of(jnp.where(even, HALO - BACK, HALO + count), 16)
    loads = [
        (conv_hbm.at[0], conv_ref.at[0]),
        (clip_ref, h0.at[HALO : HALO + count]),
        (clip_a_ref, h0.at[pl.ds(above, HALO)]),
        (clip_b_ref, h0.at[pl.ds(below, HALO)]),
        (conv_hbm.at[1:3], conv_ref.at[1:3]),
        (head_hbm, head_ref),
        (proj_ref, err.at[HALO : HALO + count]),
        (proj_a_ref, err.at[pl.ds(err_above, BACK)]),
        (proj_b_ref, err.at[pl.ds(err_below, BACK)]),
        (target_hbm, target_ref),
    ]
    loads = [pltpu.make_async_copy(*load, in_sem.at[i]) for i, load in enumerate(loads)]
    for load in loads:
        load.start()

    half = keep_ref.shape[1]
    stores = []

    def store(first_lane, lanes):
        for pen in range(keep_ref.shape[0]):
            for side, target in enumerate((keep_ref, send_ref)):
                start = pl.multiple_of((2 * pen + (place_ref[0] + side) % 2) * half, 8)
                copy = pltpu.make_async_copy(
                    sums.at[pl.ds(start, half), first_lane : first_lane + lanes],
                    target.at[pen, :, first_lane : first_lane + lanes],
                    out_sem.at[len(stores)],
                )
                copy.start()
                stores.append(copy)

    for load in loads[:4]:
        load.wait()
    reach = HALO
    for layer in range(3):
        width = DILATIONS[layer]
        reach -= width
        source, result, slope = hidden[layer], hidden[layer + 1], slopes[layer + 1]
        weights = conv_ref[layer].reshape(3 * W, W)

        def forward(frame, size):
            taps = [source[at(frame + (k - 1) * width, size), :] for k in range(3)]
            pre = dot(jnp.concatenate(taps, axis=1), weights)
            sig = 0.5 * jnp.tanh(0.5 * pre) + 0.5
            new = taps[1].astype(jnp.float32) + pre * sig
            result[at(frame, size), :] = masked(frame, size, new).astype(jnp.bfloat16)
            slope[at(frame, size), :] = sig * (1.0 + pre * (1.0 - sig))

        loop_rows(-reach, count + reach, 416, forward)
        if layer == 0:
            loads[4].wait()
            for turn in (1, 2):
                for k in range(3):
                    turned = jnp.transpose(conv_ref[turn, k])
                    conv_t[turn - 1, 2 * k * W : (2 * k + 1) * W, :] = turned
                    conv_t[turn - 1, (2 * k + 1) * W : (2 * k + 2) * W, :] = turned

    def store_back(frame, size, error, slope):
        high, low = split(error * slope[at(frame, size), :])
        back[at(frame, size), 0:W] = high
        back[at(frame, size), W : 2 * W] = low

    def head_error(frame, size):
        top = h3[at(frame, size), :]
        error = SCALE * (dot(jnp.concatenate([top, top], axis=1), gram[...]) - err[at(frame, size), :])
        err[at(frame, size), :] = error
        store_back(frame, size, error, s3)

    for load in loads[5:9]:
        load.wait()
    high, low = split(dot_nt(head_ref[...], head_ref[...]))
    gram[0:W, :] = high
    gram[W : 2 * W, :] = low
    loop_rows(-BACK, count + BACK, 416, head_error)

    loads[9].wait()
    top = h3[at(0, count), :]
    head_acc[...] = dot_tn(top, target_ref[...])
    square = dot_tn(top, top)
    high = square.astype(jnp.bfloat16)
    middle, low = split(square - high.astype(jnp.float32))
    weight = head_ref[...]
    product = dot(high, weight) + (dot(middle, weight) + dot(low, weight))
    sums[:, 9 * W :] = SCALE * (product - head_acc[...])
    store(9 * W, FEAT)

    reach = BACK
    for layer in (2, 1, 0):
        width = DILATIONS[layer]
        source = hidden[layer]
        first_lane = 3 * layer * W
        right = back[at(0, count), :]
        for k in range(3):
            both = dot_tn(source[at((k - 1) * width, count), :], right)
            sums[:, first_lane + k * W : first_lane + (k + 1) * W] = both[:, 0:W] + both[:, W:]
        store(first_lane, 3 * W)
        if layer > 0:
            reach -= width

            def pull_back(frame, size):
                taps = [back[at(frame - (k - 1) * width, size), :] for k in range(3)]
                err[at(frame, size), :] += dot(jnp.concatenate(taps, axis=1), conv_t[layer - 1])

            loop_rows(-reach, count + reach, 416, pull_back)

            def slope_back(frame, size):
                error = masked(frame, size, err[at(frame, size), :])
                store_back(frame, size, error, slopes[layer])

            loop_rows(-reach, count + reach, 416, slope_back)
    for copy in stores:
        copy.wait()


def main(pens, place, clip, clip_a, clip_b, target, proj, proj_a, proj_b, conv_weight, head_weight):
    count = clip.shape[0]
    rows = count + 2 * HALO
    flops = 2 * W * W * (9 * rows + 14 * rows + 18 * count + 6 * count)
    return pl.pallas_call(
        functools.partial(main_kernel, count),
        in_specs=[smem()] + [pl.BlockSpec(memory_space=pl.ANY)] * 9,
        out_specs=[pl.BlockSpec(memory_space=pl.ANY)] * 2,
        out_shape=[jax.ShapeDtypeStruct((pens, W // (2 * pens), SUM_LANES), jnp.float32)] * 2,
        scratch_shapes=[pltpu.VMEM((rows, W), jnp.bfloat16)] * 4
        + [pltpu.VMEM((rows, W), jnp.float32)] * 4
        + [
            pltpu.VMEM((rows, 2 * W), jnp.bfloat16),
            pltpu.VMEM((2, 6 * W, W), jnp.bfloat16),
            pltpu.VMEM((2 * W, W), jnp.bfloat16),
            pltpu.VMEM((W, FEAT), jnp.float32),
            pltpu.VMEM((W, SUM_LANES), jnp.float32),
            pltpu.VMEM(conv_weight.shape, jnp.bfloat16),
            pltpu.VMEM(head_weight.shape, jnp.bfloat16),
            pltpu.VMEM(target.shape, jnp.bfloat16),
            pltpu.SemaphoreType.DMA((10,)),
            pltpu.SemaphoreType.DMA((8 * pens,)),
        ],
        compiler_params=pltpu.CompilerParams(vmem_limit_bytes=56 * 2**20),
        cost_estimate=pl.CostEstimate(flops=flops, bytes_accessed=16 * 2**20, transcendentals=3 * rows * W),
        name="forward_backward",
    )(place, clip, clip_a, clip_b, target, proj, proj_a, proj_b, conv_weight, head_weight)


def swap(near, far):
    count = lax.axis_size("tm")
    pairs = [(i, i + 1) for i in range(1, count - 1, 2)]
    from_far = lax.ppermute(far, "tm", pairs + [(j, i) for i, j in pairs])
    return lax.ppermute(near, "tm", [(i, i ^ 1) for i in range(count)]), from_far


def encode(values, code_ref):
    pens = len(values)
    for place, (first, stop) in enumerate(GROUPS):
        lanes = range(first, stop, 128)
        most = functools.reduce(
            jnp.maximum, [jnp.abs(values[pen][:, lane : lane + 128]) for pen in range(pens) for lane in lanes]
        )
        most = (most * 1.0079).astype(jnp.bfloat16)
        code_ref[place, :, SUM_LANES:] = most
        most = most.astype(jnp.float32)
        grow = jnp.where(most > 1e-36, SPAN / jnp.maximum(most, 1e-36), 0.0)
        for pen in range(pens):
            for lane in lanes:
                part = values[pen][:, lane : lane + 128]
                code = jnp.exp(jnp.abs(part) * grow - BASE)
                code = jnp.where(part < 0.0, -code, code)
                code_ref[pen, :, lane : lane + 128] = code.astype(jnp.bfloat16)
    for pen in range(len(GROUPS), pens):
        code_ref[pen, :, SUM_LANES:] = jnp.zeros_like(code_ref[pen, :, SUM_LANES:])


def decode(code_ref, pen, lane, place):
    code = code_ref[pen, :, lane : lane + 128].astype(jnp.float32)
    most = code_ref[place, :, SUM_LANES:].astype(jnp.float32) * (1.0 / SPAN)
    size = (jnp.log(jnp.abs(code)) + BASE) * most
    return jnp.where(code < 0.0, -size, size)


def cores_kernel(place_ref, keep_ref, other_ref, own_ref, *sent):
    groups, pens, rows = len(sent) + 1, own_ref.shape[0], own_ref.shape[1]
    group = place_ref[0] // 2

    def rows_of(index, pen):
        if rows % 8 == 0:
            here = pl.ds(pl.multiple_of(index * rows, 8), rows)
            return keep_ref[pen, here, :] + other_ref[pen, here, :]
        total = keep_ref[pen] + other_ref[pen]
        return functools.reduce(
            lambda a, b: a + b,
            [jnp.where(index == i, total[i * rows : (i + 1) * rows], 0.0) for i in range(groups)],
        )

    for pen in range(pens):
        own_ref[pen] = rows_of(group, pen)
    for j in range(1, groups):
        encode([rows_of(group ^ j, pen) for pen in range(pens)], sent[j - 1])


def chips_kernel(place_ref, own_ref, *refs):
    pens = own_ref.shape[0]
    arrived, mine_ref, sent = refs[:-2], refs[-2], refs[-1]
    for place, (first, stop) in enumerate(GROUPS):
        for lane in range(first, stop, 128):
            for pen in range(pens):
                total = own_ref[pen, :, lane : lane + 128]
                for other in arrived:
                    total = total + decode(other, pen, lane, place)
                sent[pen, :, lane : lane + 128] = total
    mine_ref[...] = sent[place_ref[2]]


def smem():
    return pl.BlockSpec(memory_space=pltpu.SMEM)


def whole():
    return pl.BlockSpec(memory_space=pltpu.VMEM)


def sum_cores(place, keep, other, groups):
    pens, half, lanes = keep.shape
    rows = half // groups
    return pl.pallas_call(
        cores_kernel,
        in_specs=[smem()] + [whole()] * 2,
        out_specs=[whole()] * groups,
        out_shape=[jax.ShapeDtypeStruct((pens, rows, lanes), jnp.float32)]
        + [jax.ShapeDtypeStruct((pens, rows, CODE_LANES), jnp.bfloat16)] * (groups - 1),
        name="sum_cores",
    )(place, keep, other)


def sum_chips(place, own, arrived):
    pens, rows, lanes = own.shape
    def kernel(place_ref, *refs):
        ins, outs, total = refs[: 1 + len(arrived)], refs[1 + len(arrived) : -1], refs[-1]
        chips_kernel(place_ref, *ins, outs[0], total)
        for j in range(1, pens):
            outs[j][...] = total[place_ref[2] ^ j]

    return pl.pallas_call(
        kernel,
        in_specs=[smem()] + [whole()] * (1 + len(arrived)),
        out_specs=[whole()] * pens,
        out_shape=[jax.ShapeDtypeStruct((rows, lanes), jnp.float32)] * pens,
        scratch_shapes=[pltpu.VMEM((pens, rows, lanes), jnp.float32)],
        name="sum_chips",
    )(place, own, *arrived)


def reduce_sums(place, keep, send):
    n, pens = lax.axis_size("tm"), lax.axis_size("pen")
    groups = n // 2
    sibling = [(i, i ^ 1) for i in range(n)]
    chips = [[(i, i ^ (2 * j)) for i in range(n)] for j in range(1, groups)]
    streams = [[(i, i ^ j) for i in range(pens)] for j in range(1, pens)]
    other = lax.ppermute(send, "tm", sibling)
    own, *codes = sum_cores(place, keep, other, groups)
    arrived = [lax.ppermute(code, "tm", pairs) for code, pairs in zip(codes, chips)]
    mine, *parts = sum_chips(place, own, arrived)
    for part, pairs in zip(parts, streams):
        mine = mine + lax.ppermute(part, "pen", pairs)
    core, group = place[0] % 2, place[0] // 2
    half = jnp.zeros((groups,) + mine.shape, mine.dtype)
    half = lax.dynamic_update_index_in_dim(half, mine, group, 0)
    for j, pairs in enumerate(chips, 1):
        half = lax.dynamic_update_index_in_dim(half, lax.ppermute(mine, "tm", pairs), group ^ j, 0)
    half = half.reshape(-1, half.shape[2])
    other = lax.ppermute(half, "tm", sibling)
    rows = jnp.concatenate([jnp.where(core == 0, half, other), jnp.where(core == 0, other, half)], axis=0)
    return rows[:, : 9 * W].reshape(-1, 3, 3, W).transpose(1, 2, 0, 3), rows[:, 9 * W :]


def on_device(clips, targets, conv_weight, head_weight):
    clip, target = clips[0], targets[0]
    count, pens = lax.axis_size("tm"), lax.axis_size("pen")
    place = jnp.stack([lax.axis_index("tm"), count, lax.axis_index("pen"), pens]).astype(jnp.int32)
    even = place[0] % 2 == 0
    low, high = clip[:HALO], clip[clip.shape[0] - HALO :]
    clip_a, clip_b = swap(jnp.where(even, high, low), jnp.where(even, low, high))
    proj, near, far = project(place, target, head_weight)
    proj_a, proj_b = swap(near, far)
    keep, send = main(
        pens, place, clip, clip_a, clip_b, target, proj, proj_a, proj_b, conv_weight, head_weight
    )
    return reduce_sums(place, keep, send)


def solution(mesh):
    in_specs = (P("pen", "tm", None), P("pen", "tm", None), P(), P())
    out_specs = (P(None, None, "pen", None), P("pen", None))
    return jax.shard_map(
        on_device, mesh=mesh, in_specs=in_specs, out_specs=out_specs, check_vma=False
    )
```

```python
import functools
import math

import jax
import jax.numpy as jnp
from jax import lax
from jax.experimental import pallas as pl
from jax.experimental.pallas import tpu as pltpu
from jax.sharding import PartitionSpec as P

W = 256
FEAT = 1024
DILATIONS = (16, 64, 256)
BACK = DILATIONS[1] + DILATIONS[2]
HALO = BACK + sum(DILATIONS)
SCALE = 2.0 / FEAT
SUM_LANES = 9 * W + FEAT
GROUPS = ((0, 3 * W), (3 * W, 6 * W), (6 * W, 9 * W), (9 * W, SUM_LANES))
CODE_LANES = SUM_LANES + 128 * 4
VMEM_LIMIT = 52 * 2**20
BASE = 125.0 * math.log(2.0)
SPAN = 250.0 * math.log(2.0)


def dot(left, right):
    return lax.dot_general(
        left, right, (((1,), (0,)), ((), ())), preferred_element_type=jnp.float32
    )


def dot_nt(left, right):
    return lax.dot_general(
        left, right, (((1,), (1,)), ((), ())), preferred_element_type=jnp.float32
    )


def dot_tn(left, right):
    return lax.dot_general(
        left, right, (((0,), (0,)), ((), ())), preferred_element_type=jnp.float32
    )


def split(value):
    high = value.astype(jnp.bfloat16)
    return high, (value - high.astype(jnp.float32)).astype(jnp.bfloat16)


def tile_of(rows, most):
    best = 16
    for size in range(16, most + 1, 16):
        if rows % size == 0:
            best = size
    return best


def loop_rows(start, stop, most, body):
    tile = tile_of(stop - start, most)
    for frame in range(start, stop, tile):
        body(frame, tile)


def edges_kernel(place_ref, clip_hbm, target_hbm, head_ref, near_ref, far_ref, goal_ref, sem):
    count = clip_hbm.shape[0]
    even = place_ref[0] % 2 == 0
    loads = []
    for side, (edge_ref, flag) in enumerate(((near_ref, even), (far_ref, jnp.logical_not(even)))):
        for rows, source, target in (
            (BACK, target_hbm, goal_ref.at[side * BACK : (side + 1) * BACK]),
            (HALO, clip_hbm, edge_ref.at[0:HALO]),
        ):
            start = pl.multiple_of(jnp.where(flag, count - rows, 0), 16)
            loads.append(pltpu.make_async_copy(source.at[pl.ds(start, rows)], target, sem.at[len(loads)]))
            loads[-1].start()
    for side, edge_ref in enumerate((near_ref, far_ref)):
        loads[2 * side].wait()
        high, low = split(dot_nt(goal_ref[side * BACK : (side + 1) * BACK], head_ref[...]))
        edge_ref[HALO : HALO + BACK] = high
        edge_ref[HALO + BACK :] = low
    for load in loads[1::2]:
        load.wait()


def edges(place, clip, target, head_weight):
    anywhere = pl.BlockSpec(memory_space=pl.ANY)
    return pl.pallas_call(
        edges_kernel,
        in_specs=[smem(), anywhere, anywhere, whole()],
        out_specs=[whole()] * 2,
        out_shape=[jax.ShapeDtypeStruct((HALO + 2 * BACK, W), jnp.bfloat16)] * 2,
        scratch_shapes=[pltpu.VMEM((2 * BACK, FEAT), jnp.bfloat16), pltpu.SemaphoreType.DMA((4,))],
        compiler_params=pltpu.CompilerParams(vmem_limit_bytes=VMEM_LIMIT),
        name="edges",
    )(place, clip, target, head_weight)


def project_kernel(target_ref, head_ref, out_ref):
    out_ref[...] = dot_nt(target_ref[...], head_ref[...])


def project(target, head_weight):
    count = target.shape[0]
    tile = tile_of(count, 512)
    return pl.pallas_call(
        project_kernel,
        grid=(count // tile,),
        in_specs=[
            pl.BlockSpec((tile, FEAT), lambda i: (i, 0)),
            pl.BlockSpec((W, FEAT), lambda i: (0, 0)),
        ],
        out_specs=pl.BlockSpec((tile, W), lambda i: (i, 0)),
        out_shape=jax.ShapeDtypeStruct((count, W), jnp.float32),
        compiler_params=pltpu.CompilerParams(vmem_limit_bytes=VMEM_LIMIT),
        cost_estimate=pl.CostEstimate(
            flops=2 * count * W * FEAT, bytes_accessed=count * (2 * FEAT + 4 * W), transcendentals=0
        ),
        name="project_targets",
    )(target, head_weight)


def main_kernel(
    count,
    place_ref,
    clip_ref,
    near_ref,
    far_ref,
    target_hbm,
    proj_ref,
    conv_hbm,
    head_hbm,
    keep_ref,
    send_ref,
    h0,
    h1,
    h2,
    h3,
    s1,
    s2,
    s3,
    err,
    back,
    conv_t,
    gram,
    head_acc,
    sums,
    conv_ref,
    head_ref,
    target_ref,
    goals,
    in_sem,
    out_sem,
):
    first = place_ref[0] == 0
    last = place_ref[0] == place_ref[1] - 1
    even = place_ref[0] % 2 == 0
    hidden = (h0, h1, h2, h3)
    slopes = (None, s1, s2, s3)

    def at(frame, size):
        return slice(frame + HALO, frame + HALO + size)

    def inside(frame, size):
        rows = lax.broadcasted_iota(jnp.int32, (size, 1), 0) + frame
        return ((rows >= 0) | jnp.logical_not(first)) & ((rows < count) | jnp.logical_not(last))

    def masked(frame, size, value):
        if frame >= 0 and frame + size <= count:
            return value
        return jnp.where(inside(frame, size), value, 0.0)

    above = pl.multiple_of(jnp.where(even, HALO + count, 0), 16)
    below = pl.multiple_of(jnp.where(even, 0, HALO + count), 16)
    err_above = pl.multiple_of(jnp.where(even, HALO + count, HALO - BACK), 16)
    err_below = pl.multiple_of(jnp.where(even, HALO - BACK, HALO + count), 16)
    loads = [
        (conv_hbm.at[0], conv_ref.at[0]),
        (clip_ref, h0.at[HALO : HALO + count]),
        (near_ref.at[0:HALO], h0.at[pl.ds(above, HALO)]),
        (far_ref.at[0:HALO], h0.at[pl.ds(below, HALO)]),
        (conv_hbm.at[1:3], conv_ref.at[1:3]),
        (head_hbm, head_ref),
        (proj_ref, err.at[HALO : HALO + count]),
        (near_ref.at[HALO:], goals.at[0]),
        (far_ref.at[HALO:], goals.at[1]),
        (target_hbm, target_ref),
    ]
    loads = [pltpu.make_async_copy(*load, in_sem.at[i]) for i, load in enumerate(loads)]
    for load in loads:
        load.start()

    half = keep_ref.shape[1]
    stores = []

    def store(first_lane, lanes):
        for pen in range(keep_ref.shape[0]):
            for side, target in enumerate((keep_ref, send_ref)):
                start = pl.multiple_of((2 * pen + (place_ref[0] + side) % 2) * half, 8)
                copy = pltpu.make_async_copy(
                    sums.at[pl.ds(start, half), first_lane : first_lane + lanes],
                    target.at[pen, :, first_lane : first_lane + lanes],
                    out_sem.at[len(stores)],
                )
                copy.start()
                stores.append(copy)

    for load in loads[:4]:
        load.wait()
    reach = HALO
    for layer in range(3):
        width = DILATIONS[layer]
        reach -= width
        source, result, slope = hidden[layer], hidden[layer + 1], slopes[layer + 1]
        weights = conv_ref[layer].reshape(3 * W, W)

        def forward(frame, size):
            taps = [source[at(frame + (k - 1) * width, size), :] for k in range(3)]
            pre = dot(jnp.concatenate(taps, axis=1), weights)
            sig = 0.5 * jnp.tanh(0.5 * pre) + 0.5
            new = taps[1].astype(jnp.float32) + pre * sig
            result[at(frame, size), :] = masked(frame, size, new).astype(jnp.bfloat16)
            slope[at(frame, size), :] = sig * (1.0 + pre * (1.0 - sig))

        loop_rows(-reach, count + reach, 416, forward)
        if layer == 0:
            loads[4].wait()
            for turn in (1, 2):
                for k in range(3):
                    turned = jnp.transpose(conv_ref[turn, k])
                    conv_t[turn - 1, 2 * k * W : (2 * k + 1) * W, :] = turned
                    conv_t[turn - 1, (2 * k + 1) * W : (2 * k + 2) * W, :] = turned

    def store_back(frame, size, error, slope):
        high, low = split(error * slope[at(frame, size), :])
        back[at(frame, size), 0:W] = high
        back[at(frame, size), W : 2 * W] = low

    def head_error(frame, size):
        top = h3[at(frame, size), :]
        error = SCALE * (dot(jnp.concatenate([top, top], axis=1), gram[...]) - err[at(frame, size), :])
        err[at(frame, size), :] = error
        store_back(frame, size, error, s3)

    for load in loads[5:9]:
        load.wait()
    for side, start in enumerate((err_above, err_below)):
        high, low = goals[side, 0:BACK, :], goals[side, BACK:, :]
        err[pl.ds(start, BACK), :] = high.astype(jnp.float32) + low.astype(jnp.float32)
    high, low = split(dot_nt(head_ref[...], head_ref[...]))
    gram[0:W, :] = high
    gram[W : 2 * W, :] = low
    loop_rows(-BACK, count + BACK, 416, head_error)

    loads[9].wait()
    top = h3[at(0, count), :]
    head_acc[...] = dot_tn(top, target_ref[...])
    square = dot_tn(top, top)
    high = square.astype(jnp.bfloat16)
    middle, low = split(square - high.astype(jnp.float32))
    weight = head_ref[...]
    product = dot(high, weight) + (dot(middle, weight) + dot(low, weight))
    sums[:, 9 * W :] = SCALE * (product - head_acc[...])
    store(9 * W, FEAT)

    reach = BACK
    for layer in (2, 1, 0):
        width = DILATIONS[layer]
        source = hidden[layer]
        first_lane = 3 * layer * W
        right = back[at(0, count), :]
        for k in range(3):
            both = dot_tn(source[at((k - 1) * width, count), :], right)
            sums[:, first_lane + k * W : first_lane + (k + 1) * W] = both[:, 0:W] + both[:, W:]
        store(first_lane, 3 * W)
        if layer > 0:
            reach -= width

            def pull_back(frame, size):
                taps = [back[at(frame - (k - 1) * width, size), :] for k in range(3)]
                err[at(frame, size), :] += dot(jnp.concatenate(taps, axis=1), conv_t[layer - 1])

            loop_rows(-reach, count + reach, 416, pull_back)

            def slope_back(frame, size):
                error = masked(frame, size, err[at(frame, size), :])
                store_back(frame, size, error, slopes[layer])

            loop_rows(-reach, count + reach, 416, slope_back)
    for copy in stores:
        copy.wait()


def main(pens, place, clip, near, far, target, proj, conv_weight, head_weight):
    count = clip.shape[0]
    rows = count + 2 * HALO
    flops = 2 * W * W * (9 * rows + 14 * rows + 18 * count + 6 * count)
    return pl.pallas_call(
        functools.partial(main_kernel, count),
        in_specs=[smem()] + [pl.BlockSpec(memory_space=pl.ANY)] * 7,
        out_specs=[pl.BlockSpec(memory_space=pl.ANY)] * 2,
        out_shape=[jax.ShapeDtypeStruct((pens, W // (2 * pens), SUM_LANES), jnp.float32)] * 2,
        scratch_shapes=[pltpu.VMEM((rows, W), jnp.bfloat16)] * 4
        + [pltpu.VMEM((rows, W), jnp.float32)] * 4
        + [
            pltpu.VMEM((rows, 2 * W), jnp.bfloat16),
            pltpu.VMEM((2, 6 * W, W), jnp.bfloat16),
            pltpu.VMEM((2 * W, W), jnp.bfloat16),
            pltpu.VMEM((W, FEAT), jnp.float32),
            pltpu.VMEM((W, SUM_LANES), jnp.float32),
            pltpu.VMEM(conv_weight.shape, jnp.bfloat16),
            pltpu.VMEM(head_weight.shape, jnp.bfloat16),
            pltpu.VMEM(target.shape, jnp.bfloat16),
            pltpu.VMEM((2, 2 * BACK, W), jnp.bfloat16),
            pltpu.SemaphoreType.DMA((10,)),
            pltpu.SemaphoreType.DMA((8 * pens,)),
        ],
        compiler_params=pltpu.CompilerParams(vmem_limit_bytes=VMEM_LIMIT),
        cost_estimate=pl.CostEstimate(flops=flops, bytes_accessed=16 * 2**20, transcendentals=3 * rows * W),
        name="forward_backward",
    )(place, clip, near, far, target, proj, conv_weight, head_weight)


def swap(near, far):
    count = lax.axis_size("tm")
    pairs = [(i, i + 1) for i in range(1, count - 1, 2)]
    from_far = lax.ppermute(far, "tm", pairs + [(j, i) for i, j in pairs])
    return lax.ppermute(near, "tm", [(i, i ^ 1) for i in range(count)]), from_far


def encode(parts):
    most = functools.reduce(jnp.maximum, [jnp.abs(part) for part in parts])
    most = (most * 1.0079).astype(jnp.bfloat16)
    wide = most.astype(jnp.float32)
    grow = jnp.where(wide > 1e-36, SPAN / jnp.maximum(wide, 1e-36), 0.0)
    codes = []
    for part in parts:
        code = jnp.exp(jnp.abs(part) * grow - BASE)
        codes.append(jnp.where(part < 0.0, -code, code).astype(jnp.bfloat16))
    return codes, most


def decode(code, most):
    code = code.astype(jnp.float32)
    size = (jnp.log(jnp.abs(code)) + BASE) * (most.astype(jnp.float32) * (1.0 / SPAN))
    return jnp.where(code < 0.0, -size, size)


def tiles_of(group):
    return [slice(lane, lane + 128) for lane in range(*GROUPS[group], 128)]


def tail_of(group):
    return slice(SUM_LANES + 128 * group, SUM_LANES + 128 * (group + 1))


def encode_rows(ref, code_ref):
    for group in range(len(GROUPS)):
        tiles = tiles_of(group)
        codes, most = encode([ref[:, tile] for tile in tiles])
        for tile, code in zip(tiles, codes):
            code_ref[:, tile] = code
        code_ref[:, tail_of(group)] = most


def cores_kernel(place_ref, keep_ref, other_ref, own_ref, *sent):
    groups, pens, rows = len(sent) + 1, own_ref.shape[0], own_ref.shape[1]
    mine = place_ref[0] // 2

    def rows_of(index, pen, tile):
        if rows % 8 == 0:
            here = pl.ds(pl.multiple_of(index * rows, 8), rows)
            return keep_ref[pen, here, tile] + other_ref[pen, here, tile]
        total = keep_ref[pen, :, tile] + other_ref[pen, :, tile]
        return functools.reduce(
            lambda a, b: a + b,
            [jnp.where(index == i, total[i * rows : (i + 1) * rows], 0.0) for i in range(groups)],
        )

    for group in range(len(GROUPS)):
        places = [(pen, tile) for pen in range(pens) for tile in tiles_of(group)]
        for pen, tile in places:
            own_ref[pen, :, tile] = rows_of(mine, pen, tile)
        for j in range(1, groups):
            codes, most = encode([rows_of(mine ^ j, pen, tile) for pen, tile in places])
            for (pen, tile), code in zip(places, codes):
                sent[j - 1][pen, :, tile] = code
            sent[j - 1][group, :, SUM_LANES:] = most
    for pen in range(len(GROUPS), pens):
        for code_ref in sent:
            code_ref[pen, :, SUM_LANES:] = jnp.zeros_like(code_ref[pen, :, SUM_LANES:])


def chips_kernel(place_ref, own_ref, *refs):
    pens = own_ref.shape[0]
    arrived, mine_ref, sent, total_ref = refs[: -pens - 1], refs[-pens - 1], refs[-pens:-1], refs[-1]
    for group in range(len(GROUPS)):
        for tile in tiles_of(group):
            for pen in range(pens):
                total = own_ref[pen, :, tile]
                for other in arrived:
                    total = total + decode(other[pen, :, tile], other[group, :, SUM_LANES:])
                total_ref[pen, :, tile] = total
    mine_ref[...] = total_ref[place_ref[2]]
    for j, code_ref in enumerate(sent, 1):
        encode_rows(total_ref.at[place_ref[2] ^ j], code_ref)


def streams_kernel(mine_ref, *refs):
    arrived, code_ref, total_ref = refs[:-2], refs[-2], refs[-1]
    for group in range(len(GROUPS)):
        for tile in tiles_of(group):
            total = mine_ref[:, tile]
            for other in arrived:
                total = total + decode(other[:, tile], other[:, tail_of(group)])
            total_ref[:, tile] = total
    encode_rows(total_ref, code_ref)


def unpack_kernel(place_ref, *refs):
    codes, (conv_ref, head_ref) = refs[:-2], refs[-2:]
    groups, rows = len(codes) // 2, codes[0].shape[0]
    core, mine = place_ref[0] % 2, place_ref[0] // 2

    def write(code_ref, here):
        for group in range(len(GROUPS)):
            for tile in tiles_of(group):
                value = decode(code_ref[:, tile], code_ref[:, tail_of(group)])
                if group < 3:
                    tap, lane = (tile.start - GROUPS[group][0]) // W, tile.start % W
                    conv_ref[group, tap, here, lane : lane + 128] = value
                else:
                    lane = tile.start - GROUPS[3][0]
                    head_ref[here, lane : lane + 128] = value

    for side in range(2):
        for j in range(groups):
            code_ref = codes[side * groups + j]
            index = (core ^ side) * groups + (mine ^ j)
            if rows % 8 == 0:
                write(code_ref, pl.ds(pl.multiple_of(index * rows, 8), rows))
            else:
                for known in range(2 * groups):

                    @pl.when(index == known)
                    def _():
                        write(code_ref, slice(known * rows, (known + 1) * rows))


def smem():
    return pl.BlockSpec(memory_space=pltpu.SMEM)


def whole():
    return pl.BlockSpec(memory_space=pltpu.VMEM)


def near(arrays):
    return [pltpu.with_memory_space_constraint(array, pltpu.VMEM) for array in arrays]


def on_vmem():
    return pltpu.CompilerParams(vmem_limit_bytes=16 * 2**20)


def sum_cores(place, keep, other, groups):
    pens, half, lanes = keep.shape
    rows = half // groups
    return pl.pallas_call(
        cores_kernel,
        in_specs=[smem(), whole(), whole()],
        out_specs=[whole()] * groups,
        out_shape=[jax.ShapeDtypeStruct((pens, rows, lanes), jnp.float32)]
        + [jax.ShapeDtypeStruct((pens, rows, lanes + 128), jnp.bfloat16)] * (groups - 1),
        compiler_params=on_vmem(),
        name="sum_cores",
    )(place, *near([keep, other]))


def sum_chips(place, own, arrived):
    pens, rows, lanes = own.shape
    return pl.pallas_call(
        chips_kernel,
        in_specs=[smem()] + [whole()] * (1 + len(arrived)),
        out_specs=[whole()] * pens,
        out_shape=[jax.ShapeDtypeStruct((rows, lanes), jnp.float32)]
        + [jax.ShapeDtypeStruct((rows, CODE_LANES), jnp.bfloat16)] * (pens - 1),
        scratch_shapes=[pltpu.VMEM(own.shape, jnp.float32)],
        compiler_params=on_vmem(),
        name="sum_chips",
    )(place, *near([own] + arrived))


def sum_streams(mine, arrived):
    return pl.pallas_call(
        streams_kernel,
        in_specs=[whole()] * (1 + len(arrived)),
        out_specs=whole(),
        out_shape=jax.ShapeDtypeStruct((mine.shape[0], CODE_LANES), jnp.bfloat16),
        scratch_shapes=[pltpu.VMEM(mine.shape, jnp.float32)],
        compiler_params=on_vmem(),
        name="sum_streams",
    )(*near([mine] + arrived))


def unpack(place, codes):
    rows = len(codes) * codes[0].shape[0]
    return pl.pallas_call(
        unpack_kernel,
        in_specs=[smem()] + [whole()] * len(codes),
        out_specs=[whole()] * 2,
        out_shape=[
            jax.ShapeDtypeStruct((3, 3, rows, W), jnp.float32),
            jax.ShapeDtypeStruct((rows, FEAT), jnp.float32),
        ],
        compiler_params=on_vmem(),
        name="unpack",
    )(place, *near(codes))


def reduce_sums(place, keep, send):
    n, pens = lax.axis_size("tm"), lax.axis_size("pen")
    groups = n // 2
    sibling = [(i, i ^ 1) for i in range(n)]
    chips = [[(i, i ^ (2 * j)) for i in range(n)] for j in range(1, groups)]
    streams = [[(i, i ^ j) for i in range(pens)] for j in range(1, pens)]
    other = lax.ppermute(send, "tm", sibling)
    own, *codes = sum_cores(place, keep, other, groups)
    arrived = [lax.ppermute(code, "tm", pairs) for code, pairs in zip(codes, chips)]
    mine, *codes = sum_chips(place, own, arrived)
    arrived = [lax.ppermute(code, "pen", pairs) for code, pairs in zip(codes, streams)]
    code = sum_streams(mine, arrived)
    half = [code] + [lax.ppermute(code, "tm", pairs) for pairs in chips]
    return unpack(place, half + [lax.ppermute(code, "tm", sibling) for code in half])


def on_device(clips, targets, conv_weight, head_weight):
    clip, target = clips[0], targets[0]
    count, pens = lax.axis_size("tm"), lax.axis_size("pen")
    place = jnp.stack([lax.axis_index("tm"), count, lax.axis_index("pen"), pens]).astype(jnp.int32)
    near, far = swap(*edges(place, clip, target, head_weight))
    proj = project(target, head_weight)
    keep, send = main(pens, place, clip, near, far, target, proj, conv_weight, head_weight)
    return reduce_sums(place, keep, send)


def solution(mesh):
    in_specs = (P("pen", "tm", None), P("pen", "tm", None), P(), P())
    out_specs = (P(None, None, "pen", None), P("pen", None))
    return jax.shard_map(
        on_device, mesh=mesh, in_specs=in_specs, out_specs=out_specs, check_vma=False
    )
```

```python
import functools
import math

import jax
import jax.numpy as jnp
from jax import lax
from jax.experimental import pallas as pl
from jax.experimental.pallas import tpu as pltpu
from jax.sharding import PartitionSpec as P

W = 256
FEAT = 1024
DILATIONS = (16, 64, 256)
BACK = DILATIONS[1] + DILATIONS[2]
HALO = BACK + sum(DILATIONS)
SCALE = 2.0 / FEAT
SUM_LANES = 9 * W + FEAT
GROUPS = ((0, 3 * W), (3 * W, 6 * W), (6 * W, 9 * W), (9 * W, SUM_LANES))
CODE_LANES = SUM_LANES + 128 * 4
VMEM_LIMIT = 52 * 2**20
KERNEL_LIMIT = 10 * 2**20
BASE = 125.0 * math.log(2.0)
SPAN = 250.0 * math.log(2.0)


def dot(left, right):
    return lax.dot_general(
        left, right, (((1,), (0,)), ((), ())), preferred_element_type=jnp.float32
    )


def dot_nt(left, right):
    return lax.dot_general(
        left, right, (((1,), (1,)), ((), ())), preferred_element_type=jnp.float32
    )


def dot_tn(left, right):
    return lax.dot_general(
        left, right, (((0,), (0,)), ((), ())), preferred_element_type=jnp.float32
    )


def split(value):
    high = value.astype(jnp.bfloat16)
    return high, (value - high.astype(jnp.float32)).astype(jnp.bfloat16)


def tile_of(rows, most):
    best = 16
    for size in range(16, most + 1, 16):
        if rows % size == 0:
            best = size
    return best


def loop_rows(start, stop, most, body):
    tile = tile_of(stop - start, most)
    for frame in range(start, stop, tile):
        body(frame, tile)


def edges_kernel(place_ref, clip_hbm, target_hbm, head_hbm, near_ref, far_ref, goal_ref, head_ref, sem):
    count = clip_hbm.shape[0]
    even = place_ref[0] % 2 == 0
    head_load = pltpu.make_async_copy(head_hbm, head_ref, sem.at[4])
    head_load.start()
    loads = []
    for side, (edge_ref, flag) in enumerate(((near_ref, even), (far_ref, jnp.logical_not(even)))):
        for rows, source, target in (
            (BACK, target_hbm, goal_ref.at[side * BACK : (side + 1) * BACK]),
            (HALO, clip_hbm, edge_ref.at[0:HALO]),
        ):
            start = pl.multiple_of(jnp.where(flag, count - rows, 0), 16)
            loads.append(pltpu.make_async_copy(source.at[pl.ds(start, rows)], target, sem.at[len(loads)]))
            loads[-1].start()
    head_load.wait()
    for side, edge_ref in enumerate((near_ref, far_ref)):
        loads[2 * side].wait()
        goal = dot_nt(goal_ref[side * BACK : (side + 1) * BACK], head_ref[...])
        codes, most = encode([goal[row : row + 16] for row in range(0, BACK, 16)])
        edge_ref[HALO : HALO + BACK] = jnp.concatenate(codes, axis=0)
        edge_ref[HALO + BACK :] = most
    for load in loads[1::2]:
        load.wait()


def edges(place, clip, target, head_weight):
    anywhere = pl.BlockSpec(memory_space=pl.ANY)
    return pl.pallas_call(
        edges_kernel,
        in_specs=[smem()] + [anywhere] * 3,
        out_specs=[whole()] * 2,
        out_shape=[jax.ShapeDtypeStruct((HALO + BACK + 16, W), jnp.bfloat16)] * 2,
        scratch_shapes=[
            pltpu.VMEM((2 * BACK, FEAT), jnp.bfloat16),
            pltpu.VMEM(head_weight.shape, jnp.bfloat16),
            pltpu.SemaphoreType.DMA((5,)),
        ],
        compiler_params=pltpu.CompilerParams(vmem_limit_bytes=VMEM_LIMIT),
        name="edges",
    )(place, clip, target, pltpu.with_memory_space_constraint(head_weight, pltpu.HBM))


FORWARD_EDGES = (64, 128, 384)
BACK_EDGES = {2: 384, 1: 640, 0: 704}
STATE = ("h0", "h1", "h2", "h3", "s1", "s2", "s3", "err", "back3", "back2", "sums", "goal_acc", "square")
FIXED = ("conv", "conv_t", "head", "gram")


def state_shapes(count):
    rows = count + 2 * HALO
    shapes = {name: ((rows, W), jnp.bfloat16) for name in ("h0", "h1", "h2", "h3")}
    shapes |= {name: ((rows, W), jnp.float32) for name in ("s1", "s2", "s3", "err")}
    shapes |= {name: ((rows, 2 * W), jnp.bfloat16) for name in ("back3", "back2")}
    shapes |= {
        "sums": ((W, SUM_LANES), jnp.float32),
        "goal_acc": ((W, FEAT), jnp.float32),
        "square": ((W, W), jnp.float32),
        "conv": ((3, 3, W, W), jnp.bfloat16),
        "conv_t": ((2, 6 * W, W), jnp.bfloat16),
        "head": ((W, FEAT), jnp.bfloat16),
        "gram": ((2 * W, W), jnp.bfloat16),
    }
    return {name: jax.ShapeDtypeStruct(*shape) for name, shape in shapes.items()}


def at(frame, size):
    return slice(frame + HALO, frame + HALO + size)


class Block:
    def __init__(self, count, place_ref, refs, back1, inner):
        self.count, self.refs, self.inner = count, refs, inner
        self.first = place_ref[0] == 0
        self.last = place_ref[0] == place_ref[1] - 1
        self.backs = {2: refs["back3"], 1: refs["back2"], 0: back1}

    def spans(self, reach, edge):
        if self.inner:
            return [(edge, self.count - edge)]
        return [(-reach, edge), (self.count - edge, self.count + reach)]

    def loop(self, reach, edge, body):
        for start, stop in self.spans(reach, edge):
            loop_rows(start, stop, 448, body)

    def masked(self, frame, size, value):
        if frame >= 0 and frame + size <= self.count:
            return value
        rows = lax.broadcasted_iota(jnp.int32, (size, 1), 0) + frame
        inside = (rows >= 0) | jnp.logical_not(self.first)
        inside = inside & ((rows < self.count) | jnp.logical_not(self.last))
        return jnp.where(inside, value, 0.0)

    def forward(self, layer):
        width = DILATIONS[layer]
        source, result = self.refs[f"h{layer}"], self.refs[f"h{layer + 1}"]
        slope = self.refs[f"s{layer + 1}"]
        weights = self.refs["conv"][layer].reshape(3 * W, W)

        def body(frame, size):
            taps = [source[at(frame + (k - 1) * width, size), :] for k in range(3)]
            pre = dot(jnp.concatenate(taps, axis=1), weights)
            sig = 0.5 * jnp.tanh(0.5 * pre) + 0.5
            new = taps[1].astype(jnp.float32) + pre * sig
            result[at(frame, size), :] = self.masked(frame, size, new).astype(jnp.bfloat16)
            slope[at(frame, size), :] = sig * (1.0 + pre * (1.0 - sig))

        self.loop(HALO - sum(DILATIONS[: layer + 1]), FORWARD_EDGES[layer], body)

    def store_back(self, layer, frame, size, error):
        high, low = split(error * self.refs[f"s{layer + 1}"][at(frame, size), :])
        where = at(frame, size) if layer > 0 else slice(frame, frame + size)
        self.backs[layer][where, 0:W] = high
        self.backs[layer][where, W : 2 * W] = low

    def head_error(self):
        err = self.refs["err"]

        def body(frame, size):
            top = self.refs["h3"][at(frame, size), :]
            product = dot(jnp.concatenate([top, top], axis=1), self.refs["gram"][...])
            error = SCALE * (product - err[at(frame, size), :])
            err[at(frame, size), :] = error
            self.store_back(2, frame, size, error)

        self.loop(BACK, BACK_EDGES[2], body)

    def add(self, ref, lanes, value, fresh):
        if fresh:
            ref[:, lanes] = value
        else:
            ref[:, lanes] += value

    def head_sums(self):
        goal_at = 0
        for start, stop in self.spans(0, BACK_EDGES[2]):
            goal_at = start if self.inner else goal_at
            goal = self.refs["target"][goal_at : goal_at + stop - start, :]
            goal_at += stop - start
            top = self.refs["h3"][at(start, stop - start), :]
            every = slice(None)
            self.add(self.refs["goal_acc"], every, dot_tn(top, goal), self.inner)
            self.add(self.refs["square"], every, dot_tn(top, top), self.inner)

    def weight_sums(self, layer):
        width = DILATIONS[layer]
        for start, stop in self.spans(0, BACK_EDGES[layer]):
            size = stop - start
            where = at(start, size) if layer > 0 else slice(start, stop)
            right = self.backs[layer][where, :]
            for k in range(3):
                both = dot_tn(self.refs[f"h{layer}"][at(start + (k - 1) * width, size), :], right)
                first = (3 * layer + k) * W
                self.add(self.refs["sums"], slice(first, first + W), both[:, 0:W] + both[:, W:], self.inner)

    def pull_back(self, layer):
        width = DILATIONS[layer]
        err = self.refs["err"]

        def pull(frame, size):
            taps = [self.backs[layer][at(frame - (k - 1) * width, size), :] for k in range(3)]
            error = err[at(frame, size), :] + dot(jnp.concatenate(taps, axis=1), self.refs["conv_t"][layer - 1])
            err[at(frame, size), :] = error
            self.store_back(layer - 1, frame, size, self.masked(frame, size, error))

        self.loop(BACK - sum(DILATIONS[layer:]), BACK_EDGES[layer - 1], pull)


def inner_kernel(count, place_ref, clip_hbm, target_hbm, conv_hbm, head_hbm, *rest):
    names = STATE + FIXED
    refs = dict(zip(names, rest[: len(names)]))
    back1, refs["target"], sem = rest[len(names) :]
    loads = [
        (conv_hbm.at[0], refs["conv"].at[0]),
        (clip_hbm, refs["h0"].at[HALO : HALO + count]),
        (conv_hbm.at[1:3], refs["conv"].at[1:3]),
        (head_hbm, refs["head"]),
        (target_hbm, refs["target"]),
    ]
    loads = [pltpu.make_async_copy(*load, sem.at[i]) for i, load in enumerate(loads)]
    for load in loads:
        load.start()
    block = Block(count, place_ref, refs, back1, True)
    loads[0].wait()
    loads[1].wait()
    block.forward(0)
    loads[2].wait()
    block.forward(1)
    block.forward(2)
    for layer in (1, 2):
        for k in range(3):
            turned = jnp.transpose(refs["conv"][layer, k])
            refs["conv_t"][layer - 1, 2 * k * W : (2 * k + 1) * W, :] = turned
            refs["conv_t"][layer - 1, (2 * k + 1) * W : (2 * k + 2) * W, :] = turned
    loads[3].wait()
    high, low = split(dot_nt(refs["head"][...], refs["head"][...]))
    refs["gram"][0:W, :] = high
    refs["gram"][W : 2 * W, :] = low
    loads[4].wait()

    def project(frame, size):
        refs["err"][at(frame, size), :] = dot_nt(refs["target"][frame : frame + size, :], refs["head"][...])

    loop_rows(0, count, 512, project)
    block.head_error()
    block.head_sums()
    block.weight_sums(2)
    block.pull_back(2)
    block.weight_sums(1)
    block.pull_back(1)
    block.weight_sums(0)


def inner(place, clip, target, conv_weight, head_weight):
    count = clip.shape[0]
    shapes = state_shapes(count)
    names = STATE + FIXED
    anywhere = pl.BlockSpec(memory_space=pl.ANY)
    results = pl.pallas_call(
        functools.partial(inner_kernel, count),
        in_specs=[smem()] + [anywhere] * 4,
        out_specs=[whole()] * len(names),
        out_shape=[shapes[name] for name in names],
        scratch_shapes=[
            pltpu.VMEM((count, 2 * W), jnp.bfloat16),
            pltpu.VMEM((count, FEAT), jnp.bfloat16),
            pltpu.SemaphoreType.DMA((5,)),
        ],
        compiler_params=pltpu.CompilerParams(vmem_limit_bytes=KERNEL_LIMIT),
        cost_estimate=pl.CostEstimate(flops=2 * W * W * 60 * count, bytes_accessed=8 * 2**20, transcendentals=0),
        name="inner_frames",
    )(place, *[pltpu.with_memory_space_constraint(x, pltpu.HBM) for x in (clip, target, conv_weight, head_weight)])
    return dict(zip(names, results))


def ends_kernel(count, place_ref, target_hbm, near_ref, far_ref, *rest):
    fixed = dict(zip(FIXED, rest[: len(FIXED)]))
    rest = rest[len(FIXED) + len(STATE) :]
    keep_ref, send_ref = rest[:2]
    refs = fixed | dict(zip(STATE, rest[2 : 2 + len(STATE)]))
    back1, refs["target"], in_sem = rest[2 + len(STATE) :]
    even = place_ref[0] % 2 == 0
    sums = refs["sums"]
    edge = BACK_EDGES[2]
    loads = [
        pltpu.make_async_copy(
            target_hbm.at[start : start + edge], refs["target"].at[i * edge : (i + 1) * edge], in_sem.at[i]
        )
        for i, start in enumerate((0, count - edge))
    ]
    for load in loads:
        load.start()
    for edge_ref, above in ((near_ref, even), (far_ref, jnp.logical_not(even))):
        start = pl.multiple_of(jnp.where(above, HALO + count, 0), 16)
        refs["h0"][pl.ds(start, HALO), :] = edge_ref[0:HALO, :]
        start = pl.multiple_of(jnp.where(above, HALO + count, HALO - BACK), 16)
        most = edge_ref[HALO + BACK :, :]
        for row in range(0, BACK, 16):
            code = edge_ref[HALO + row : HALO + row + 16, :]
            goal = jnp.where(code == 0.0, 0.0, decode(code, most))
            refs["err"][pl.ds(pl.multiple_of(start + row, 16), 16), :] = goal

    half = keep_ref.shape[1]

    def store(first_lane, lanes):
        part = slice(first_lane, first_lane + lanes)
        for pen in range(keep_ref.shape[0]):
            for side, target in enumerate((keep_ref, send_ref)):
                start = pl.multiple_of((2 * pen + (place_ref[0] + side) % 2) * half, 8)
                target[pen, :, part] = sums[pl.ds(start, half), part]

    block = Block(count, place_ref, refs, back1, False)
    for layer in range(3):
        block.forward(layer)
    block.head_error()
    for load in loads:
        load.wait()
    block.head_sums()
    square = refs["square"][...]
    high = square.astype(jnp.bfloat16)
    middle, low = split(square - high.astype(jnp.float32))
    weight = refs["head"][...]
    product = dot(high, weight) + (dot(middle, weight) + dot(low, weight))
    sums[:, 9 * W :] = SCALE * (product - refs["goal_acc"][...])
    store(9 * W, FEAT)
    for layer in (2, 1, 0):
        block.weight_sums(layer)
        store(3 * layer * W, 3 * W)
        if layer > 0:
            block.pull_back(layer)


def ends(pens, place, target, near_edge, far_edge, state):
    count = target.shape[0]
    shapes = state_shapes(count)
    sent = jax.ShapeDtypeStruct((pens, W // (2 * pens), SUM_LANES), jnp.float32)
    inputs = [near_edge, far_edge] + [state[name] for name in FIXED + STATE]
    first = 4 + len(FIXED)
    results = pl.pallas_call(
        functools.partial(ends_kernel, count),
        in_specs=[smem(), pl.BlockSpec(memory_space=pl.ANY)] + [whole()] * len(inputs),
        out_specs=[whole()] * (2 + len(STATE)),
        out_shape=[sent, sent] + [shapes[name] for name in STATE],
        input_output_aliases={first + i: 2 + i for i in range(len(STATE))},
        scratch_shapes=[
            pltpu.VMEM((count, 2 * W), jnp.bfloat16),
            pltpu.VMEM((2 * BACK_EDGES[2], FEAT), jnp.bfloat16),
            pltpu.SemaphoreType.DMA((2,)),
        ],
        compiler_params=pltpu.CompilerParams(vmem_limit_bytes=KERNEL_LIMIT),
        cost_estimate=pl.CostEstimate(flops=2 * W * W * 60 * count, bytes_accessed=2**20, transcendentals=0),
        name="end_frames",
    )(place, pltpu.with_memory_space_constraint(target, pltpu.HBM), *near(inputs))
    return results[:2]


def swap(near, far):
    count = lax.axis_size("tm")
    pairs = [(i, i + 1) for i in range(1, count - 1, 2)]
    from_far = lax.ppermute(far, "tm", pairs + [(j, i) for i, j in pairs])
    return lax.ppermute(near, "tm", [(i, i ^ 1) for i in range(count)]), from_far


def encode(parts):
    most = functools.reduce(jnp.maximum, [jnp.abs(part) for part in parts])
    most = (most * 1.0079).astype(jnp.bfloat16)
    wide = most.astype(jnp.float32)
    grow = jnp.where(wide > 1e-36, SPAN / jnp.maximum(wide, 1e-36), 0.0)
    codes = []
    for part in parts:
        code = jnp.exp(jnp.abs(part) * grow - BASE)
        codes.append(jnp.where(part < 0.0, -code, code).astype(jnp.bfloat16))
    return codes, most


def decode(code, most):
    code = code.astype(jnp.float32)
    size = (jnp.log(jnp.abs(code)) + BASE) * (most.astype(jnp.float32) * (1.0 / SPAN))
    return jnp.where(code < 0.0, -size, size)


def tiles_of(group):
    return [slice(lane, lane + 128) for lane in range(*GROUPS[group], 128)]


def tail_of(group):
    return slice(SUM_LANES + 128 * group, SUM_LANES + 128 * (group + 1))


def encode_rows(ref, code_ref):
    for group in range(len(GROUPS)):
        tiles = tiles_of(group)
        codes, most = encode([ref[:, tile] for tile in tiles])
        for tile, code in zip(tiles, codes):
            code_ref[:, tile] = code
        code_ref[:, tail_of(group)] = most


def cores_kernel(place_ref, keep_ref, other_ref, own_ref, *sent):
    groups, pens, rows = len(sent) + 1, own_ref.shape[0], own_ref.shape[1]
    mine = place_ref[0] // 2

    def rows_of(index, pen, tile):
        if rows % 8 == 0:
            here = pl.ds(pl.multiple_of(index * rows, 8), rows)
            return keep_ref[pen, here, tile] + other_ref[pen, here, tile]
        total = keep_ref[pen, :, tile] + other_ref[pen, :, tile]
        return functools.reduce(
            lambda a, b: a + b,
            [jnp.where(index == i, total[i * rows : (i + 1) * rows], 0.0) for i in range(groups)],
        )

    for group in range(len(GROUPS)):
        places = [(pen, tile) for pen in range(pens) for tile in tiles_of(group)]
        for pen, tile in places:
            own_ref[pen, :, tile] = rows_of(mine, pen, tile)
        for j in range(1, groups):
            codes, most = encode([rows_of(mine ^ j, pen, tile) for pen, tile in places])
            for (pen, tile), code in zip(places, codes):
                sent[j - 1][pen, :, tile] = code
            sent[j - 1][group, :, SUM_LANES:] = most
    for pen in range(len(GROUPS), pens):
        for code_ref in sent:
            code_ref[pen, :, SUM_LANES:] = jnp.zeros_like(code_ref[pen, :, SUM_LANES:])


def chips_kernel(place_ref, own_ref, *refs):
    pens = own_ref.shape[0]
    arrived, mine_ref, sent, total_ref = refs[: -pens - 1], refs[-pens - 1], refs[-pens:-1], refs[-1]
    for group in range(len(GROUPS)):
        for tile in tiles_of(group):
            for pen in range(pens):
                total = own_ref[pen, :, tile]
                for other in arrived:
                    total = total + decode(other[pen, :, tile], other[group, :, SUM_LANES:])
                total_ref[pen, :, tile] = total
    mine_ref[...] = total_ref[place_ref[2]]
    for j, code_ref in enumerate(sent, 1):
        encode_rows(total_ref.at[place_ref[2] ^ j], code_ref)


def streams_kernel(mine_ref, *refs):
    arrived, code_ref, total_ref = refs[:-2], refs[-2], refs[-1]
    for group in range(len(GROUPS)):
        for tile in tiles_of(group):
            total = mine_ref[:, tile]
            for other in arrived:
                total = total + decode(other[:, tile], other[:, tail_of(group)])
            total_ref[:, tile] = total
    encode_rows(total_ref, code_ref)


def unpack_kernel(place_ref, *refs):
    codes, (conv_ref, head_ref) = refs[:-2], refs[-2:]
    groups, rows = len(codes) // 2, codes[0].shape[0]
    core, mine = place_ref[0] % 2, place_ref[0] // 2

    def write(code_ref, here):
        for group in range(len(GROUPS)):
            for tile in tiles_of(group):
                value = decode(code_ref[:, tile], code_ref[:, tail_of(group)])
                if group < 3:
                    tap, lane = (tile.start - GROUPS[group][0]) // W, tile.start % W
                    conv_ref[group, tap, here, lane : lane + 128] = value
                else:
                    lane = tile.start - GROUPS[3][0]
                    head_ref[here, lane : lane + 128] = value

    for side in range(2):
        for j in range(groups):
            code_ref = codes[side * groups + j]
            index = (core ^ side) * groups + (mine ^ j)
            if rows % 8 == 0:
                write(code_ref, pl.ds(pl.multiple_of(index * rows, 8), rows))
            else:
                for known in range(2 * groups):

                    @pl.when(index == known)
                    def _():
                        write(code_ref, slice(known * rows, (known + 1) * rows))


def smem():
    return pl.BlockSpec(memory_space=pltpu.SMEM)


def whole():
    return pl.BlockSpec(memory_space=pltpu.VMEM)


def near(arrays):
    return [pltpu.with_memory_space_constraint(array, pltpu.VMEM) for array in arrays]


def on_vmem():
    return pltpu.CompilerParams(vmem_limit_bytes=16 * 2**20)


def sum_cores(place, keep, other, groups):
    pens, half, lanes = keep.shape
    rows = half // groups
    return pl.pallas_call(
        cores_kernel,
        in_specs=[smem(), whole(), whole()],
        out_specs=[whole()] * groups,
        out_shape=[jax.ShapeDtypeStruct((pens, rows, lanes), jnp.float32)]
        + [jax.ShapeDtypeStruct((pens, rows, lanes + 128), jnp.bfloat16)] * (groups - 1),
        compiler_params=on_vmem(),
        name="sum_cores",
    )(place, *near([keep, other]))


def sum_chips(place, own, arrived):
    pens, rows, lanes = own.shape
    return pl.pallas_call(
        chips_kernel,
        in_specs=[smem()] + [whole()] * (1 + len(arrived)),
        out_specs=[whole()] * pens,
        out_shape=[jax.ShapeDtypeStruct((rows, lanes), jnp.float32)]
        + [jax.ShapeDtypeStruct((rows, CODE_LANES), jnp.bfloat16)] * (pens - 1),
        scratch_shapes=[pltpu.VMEM(own.shape, jnp.float32)],
        compiler_params=on_vmem(),
        name="sum_chips",
    )(place, *near([own] + arrived))


def sum_streams(mine, arrived):
    return pl.pallas_call(
        streams_kernel,
        in_specs=[whole()] * (1 + len(arrived)),
        out_specs=whole(),
        out_shape=jax.ShapeDtypeStruct((mine.shape[0], CODE_LANES), jnp.bfloat16),
        scratch_shapes=[pltpu.VMEM(mine.shape, jnp.float32)],
        compiler_params=on_vmem(),
        name="sum_streams",
    )(*near([mine] + arrived))


def unpack(place, codes):
    rows = len(codes) * codes[0].shape[0]
    return pl.pallas_call(
        unpack_kernel,
        in_specs=[smem()] + [whole()] * len(codes),
        out_specs=[whole()] * 2,
        out_shape=[
            jax.ShapeDtypeStruct((3, 3, rows, W), jnp.float32),
            jax.ShapeDtypeStruct((rows, FEAT), jnp.float32),
        ],
        compiler_params=on_vmem(),
        name="unpack",
    )(place, *near(codes))


def reduce_sums(place, keep, send):
    n, pens = lax.axis_size("tm"), lax.axis_size("pen")
    groups = n // 2
    sibling = [(i, i ^ 1) for i in range(n)]
    chips = [[(i, i ^ (2 * j)) for i in range(n)] for j in range(1, groups)]
    streams = [[(i, i ^ j) for i in range(pens)] for j in range(1, pens)]
    other = lax.ppermute(send, "tm", sibling)
    own, *codes = sum_cores(place, keep, other, groups)
    arrived = [lax.ppermute(code, "tm", pairs) for code, pairs in zip(codes, chips)]
    mine, *codes = sum_chips(place, own, arrived)
    arrived = [lax.ppermute(code, "pen", pairs) for code, pairs in zip(codes, streams)]
    code = sum_streams(mine, arrived)
    half = [code] + [lax.ppermute(code, "tm", pairs) for pairs in chips]
    return unpack(place, half + [lax.ppermute(code, "tm", sibling) for code in half])


def on_device(clips, targets, conv_weight, head_weight):
    clip, target = clips[0], targets[0]
    count, pens = lax.axis_size("tm"), lax.axis_size("pen")
    place = jnp.stack([lax.axis_index("tm"), count, lax.axis_index("pen"), pens]).astype(jnp.int32)
    near_edge, far_edge = swap(*edges(place, clip, target, head_weight))
    state = inner(place, clip, target, conv_weight, head_weight)
    keep, send = ends(pens, place, target, near_edge, far_edge, state)
    return reduce_sums(place, keep, send)


def solution(mesh):
    in_specs = (P("pen", "tm", None), P("pen", "tm", None), P(), P())
    out_specs = (P(None, None, "pen", None), P("pen", None))
    return jax.shard_map(
        on_device, mesh=mesh, in_specs=in_specs, out_specs=out_specs, check_vma=False
    )
```
